32 devices in a mesh: segment: 2 (over core), tensor: 8 (over z, x), dp: 2 (over y).
Axes of the slice: x: 2, y: 2, z: 4, core: 2. Of those that a mesh axis runs over, the one named last changes fastest.
Arguments:
- tokens: bfloat16 [256, 1536], P('dp', 'tensor'), may hold values from -6 to 6
- w_gate: bfloat16 [2, 1536, 12288], P('segment', None, 'tensor'), may hold values from -0.15625 to 0.15625
- w_up: bfloat16 [2, 1536, 12288], P('segment', None, 'tensor'), may hold values from -0.15625 to 0.15625
- w_down: bfloat16 [2, 12288, 1536], P('segment', 'tensor'), may hold values from -0.0546875 to 0.0546875
- cotangent: bfloat16 [256, 1536], P('dp', 'tensor'), may hold values from -0.1796875 to 0.1796875
Outputs:
- grad_gate: float32 [2, 1536, 12288], P('segment', 'dp', 'tensor')
- grad_up: float32 [2, 1536, 12288], P('segment', 'dp', 'tensor')
- grad_down: float32 [2, 12288, 1536], P('segment', 'tensor', 'dp')
The draws below stay inside these ranges and needn't reach their ends.
All inputs are finite; a program needn't handle non-finite values.
Results may differ from the reference program's by a relative error of at most 0.023.
Values may be sent and summed in bfloat16 or wider, within the bound.
A program may use at most 64 MiB of HBM per device.

```python
import jax
import jax.numpy as jnp
from jax import lax

D = 1536
FF = 12288
TOKENS = 256
N_DP = 2


def with_spikes(array, key, source, target, parts, factor):
    owner, partner = [(jnp.arange(array.shape[dim]) // (array.shape[dim] // parts)).reshape([-1 if axis == dim else 1 for axis in range(array.ndim)]) for dim in (source, target)]
    chosen = jax.random.permutation(key, parts)[partner]
    strong = (owner == chosen) | (owner == (partner + parts // 2) % parts)
    return jnp.where(strong, factor * array, array)


def block_scale(rng, shape, shards, low, largest):
    def one(dim, shards_of):
        heights = jax.random.uniform(jax.random.fold_in(jax.random.fold_in(rng, 6), dim), (shards_of,), jnp.float32, low / len(shards), largest / len(shards))
        return jnp.repeat(jnp.exp(heights), shape[dim] // shards_of).reshape((-1,) + (1,) * (len(shape) - dim - 1))

    gain = one(*shards[0])
    for cut in shards[1:]:
        gain = gain * one(*cut)
    return gain


def normal_values(stream_key, shape, spread, bound, pieces=(), held_as=jnp.bfloat16):
    drawn = spread * jax.random.normal(stream_key, shape, jnp.float32)
    if pieces:
        drawn = drawn * block_scale(stream_key, shape, pieces, -0.22, 0.18)
    return jnp.clip(drawn, -bound, bound).astype(held_as)


def noise_with(stream_key, shape, deviation, reach, pieces, heavy, kind=jnp.bfloat16):
    entries = deviation * jax.random.normal(stream_key, shape, jnp.float32)
    if pieces:
        entries = entries * block_scale(stream_key, shape, pieces, -0.22, 0.18)
    return jnp.clip(with_spikes(entries, jax.random.fold_in(stream_key, 3), *heavy), -reach, reach).astype(kind)


def setup_inputs(seed: int = 0) -> dict:
    key_of = jax.random.split(jax.random.key(seed), 6)
    return {
        "tokens": normal_values(key_of[0], (TOKENS, D), 1.0, 6.0, ((0, 2), (1, 8))),
        "w_gate": normal_values(key_of[1], (2, D, FF), D ** -0.5, 0.15625, ((0, 2), (2, 8))),
        "w_up": normal_values(key_of[2], (2, D, FF), D ** -0.5, 0.15625, ((0, 2), (2, 8))),
        "w_down": normal_values(key_of[3], (2, FF, D), FF ** -0.5, 0.0546875, ((0, 2), (1, 8))),
        "cotangent": noise_with(key_of[4], (TOKENS, D), 0.03, 0.1796875, ((0, 2), (1, 8)), (0, 1, 8, 2.0)),
    }


def layer_forward(acts, gate_weight, up_weight, down_weight):
    gate_store = jnp.dot(acts, gate_weight, preferred_element_type=jnp.float32).astype(jnp.bfloat16)
    up_store = jnp.dot(acts, up_weight, preferred_element_type=jnp.float32).astype(jnp.bfloat16)
    gate_value = gate_store.astype(jnp.float32)
    up_value = up_store.astype(jnp.float32)
    hidden = (jax.nn.silu(gate_value) * up_value).astype(jnp.bfloat16)
    mixed_sum = jnp.dot(hidden, down_weight, preferred_element_type=jnp.float32)
    layer_out = (acts.astype(jnp.float32) + mixed_sum).astype(jnp.bfloat16)
    return layer_out, gate_value, up_value, hidden


def layer_backward(acts, gate_value, up_value, hidden, upstream, gate_weight, up_weight, down_weight):
    d_hidden = jnp.dot(upstream, down_weight.T, preferred_element_type=jnp.float32)
    sigma = jax.nn.sigmoid(gate_value)
    d_gate = (d_hidden * up_value * sigma * (1.0 + gate_value * (1.0 - sigma))).astype(jnp.bfloat16)
    d_up = (d_hidden * gate_value * sigma).astype(jnp.bfloat16)
    grad_gate = jnp.dot(acts.T, d_gate, preferred_element_type=jnp.float32)
    grad_up = jnp.dot(acts.T, d_up, preferred_element_type=jnp.float32)
    grad_down = jnp.dot(hidden.T, upstream, preferred_element_type=jnp.float32)
    inner = jnp.dot(d_gate, gate_weight.T, preferred_element_type=jnp.float32)
    inner = inner + jnp.dot(d_up, up_weight.T, preferred_element_type=jnp.float32)
    d_input = (upstream.astype(jnp.float32) + inner).astype(jnp.bfloat16)
    return d_input, grad_gate, grad_up, grad_down


def rounded(value):
    return lax.optimization_barrier(value.astype(jnp.bfloat16)).astype(jnp.float32)


def reference(tokens, w_gate, w_up, w_down, cotangent):
    per_replica = tokens.shape[0] // N_DP
    token_blocks = tokens.reshape(N_DP, per_replica, D)
    cot_blocks = cotangent.reshape(N_DP, per_replica, D)

    def replica(carry, item):
        acts, upstream = item
        middle, gate0, up0, hidden0 = layer_forward(acts, w_gate[0], w_up[0], w_down[0])
        final, gate1, up1, hidden1 = layer_forward(middle, w_gate[1], w_up[1], w_down[1])
        back1, gg1, gu1, gd1 = layer_backward(middle, gate1, up1, hidden1, upstream, w_gate[1], w_up[1], w_down[1])
        back0, gg0, gu0, gd0 = layer_backward(acts, gate0, up0, hidden0, back1, w_gate[0], w_up[0], w_down[0])
        sum_gate = carry[0] + rounded(jnp.stack([gg0, gg1]))
        sum_up = carry[1] + rounded(jnp.stack([gu0, gu1]))
        sum_down = carry[2] + rounded(jnp.stack([gd0, gd1]))
        return (sum_gate, sum_up, sum_down), None

    start = (jnp.zeros((2, D, FF), jnp.float32), jnp.zeros((2, D, FF), jnp.float32), jnp.zeros((2, FF, D), jnp.float32))
    totals, unused = lax.scan(replica, start, (token_blocks, cot_blocks))
    return totals[0], totals[1], totals[2]
```

```python
import functools

import jax
import jax.numpy as jnp
from jax import lax
from jax.experimental import pallas as pl
from jax.experimental.pallas import tpu as pltpu
from jax.sharding import PartitionSpec as P

MESH = pl.DeviceIdType.MESH
VMEM_LIMIT = 56 * 1024 * 1024


def tile_of(size):
    for tile in (512, 256, 128):
        if size % tile == 0:
            return tile
    return size


def dot(left, right):
    return jnp.dot(left, right, preferred_element_type=jnp.float32)


def dot_nt(left, right):
    return lax.dot_general(
        left, right, (((1,), (1,)), ((), ())), preferred_element_type=jnp.float32
    )


def dot_tn(left, right):
    return lax.dot_general(
        left, right, (((0,), (0,)), ((), ())), preferred_element_type=jnp.float32
    )


def hidden_of(gate, up):
    g = gate.astype(jnp.float32)
    return (g * jax.nn.sigmoid(g) * up.astype(jnp.float32)).astype(jnp.bfloat16)


def slopes(gate, up, d_hidden):
    g = gate.astype(jnp.float32)
    u = up.astype(jnp.float32)
    q = jax.nn.sigmoid(g)
    d_gate = (d_hidden * u * q * (1.0 + g * (1.0 - q))).astype(jnp.bfloat16)
    d_up = (d_hidden * g * q).astype(jnp.bfloat16)
    return d_gate, d_up


def relay_kernel(
    n, ndp, block,
    tok, cot, wg_h, wu_h, wd_h,
    a_out, b_out, h_out, dg_out, du_out,
    wg, wu, wd, shards, a_all, b_all, gate_s, up_s, hid, dgate, dup, dhid, stage, sums, turned,
    w_sem, out_sem, ag_send, ag_recv, ax_send, ax_recv, rs_send, rs_recv, bc_send, bc_recv, fw_send, fw_recv,
):
    seg = lax.axis_index("segment")
    t = lax.axis_index("tensor")
    d = lax.axis_index("dp")
    other = 1 - seg
    rows, depth = a_all.shape[1], a_all.shape[2]
    wide = hid.shape[2]
    part = tok.shape[1]
    holders = rows // block
    ff_tile, d_tile = tile_of(wide), tile_of(depth)

    loads = [
        pltpu.make_async_copy(source.at[0], target, w_sem.at[i])
        for i, (source, target) in enumerate(((wg_h, wg), (wu_h, wu), (wd_h, wd)))
    ]
    for load in loads:
        load.start()

    def place(s, x, y):
        return {"segment": s, "tensor": x, "dp": y}

    barrier = pltpu.get_barrier_semaphore()

    @pl.loop(0, n)
    def _(k):
        peer = lax.rem(t + k, n)
        pl.semaphore_signal(barrier, inc=1, device_id=place(other, peer, d), device_id_type=MESH)

        @pl.when(k > 0)
        def _():
            pl.semaphore_signal(barrier, inc=1, device_id=place(seg, peer, d), device_id_type=MESH)

    for r in range(1, ndp):
        pl.semaphore_signal(
            barrier, inc=1, device_id=place(seg, t, lax.rem(d + r, ndp)), device_id_type=MESH
        )
    shards[t] = jnp.where(seg == 0, tok[...], cot[...])
    pl.semaphore_wait(barrier, 2 * n - 1 + ndp - 1)

    def ag_copy(k, slot, peer):
        return pltpu.make_async_remote_copy(
            src_ref=shards.at[slot], dst_ref=shards.at[slot],
            send_sem=ag_send.at[k], recv_sem=ag_recv.at[k],
            device_id=place(seg, peer, d), device_id_type=MESH,
        )

    def ax_copy(r, slot):
        return pltpu.make_async_remote_copy(
            src_ref=a_all.at[slot], dst_ref=a_all.at[slot],
            send_sem=ax_send.at[r], recv_sem=ax_recv.at[r],
            device_id=place(seg, t, lax.rem(d + r, ndp)), device_id_type=MESH,
        )

    def rs_copy(k, owner, slot, peer):
        return pltpu.make_async_remote_copy(
            src_ref=stage.at[pl.ds(pl.multiple_of(owner * block, block), block)],
            dst_ref=sums.at[slot],
            send_sem=rs_send.at[k], recv_sem=rs_recv.at[k],
            device_id=place(seg, peer, d), device_id_type=MESH,
        )

    def bc_copy(k, owner, peer):
        return pltpu.make_async_remote_copy(
            src_ref=turned,
            dst_ref=b_all.at[d, pl.ds(pl.multiple_of(owner * block, block), block)],
            send_sem=bc_send.at[k], recv_sem=bc_recv.at[k],
            device_id=place(other, peer, d), device_id_type=MESH,
        )

    def fw_copy(r, k, slot, owner):
        here = b_all.at[slot, pl.ds(pl.multiple_of(owner * block, block), block)]
        return pltpu.make_async_remote_copy(
            src_ref=here, dst_ref=here,
            send_sem=fw_send.at[r, k], recv_sem=fw_recv.at[r, k],
            device_id=place(seg, t, lax.rem(d + r, ndp)), device_id_type=MESH,
        )

    def if_holder(index, action):
        if holders == n:
            action()
        else:
            pl.when(index < holders)(action)

    @pl.loop(1, n)
    def _(k):
        ag_copy(k, t, lax.rem(t + k, n)).start()

    @pl.loop(1, n)
    def _(k):
        ag_copy(k, lax.rem(t - k + n, n), t).wait_recv()

    for i in range(n):
        a_all[d, :, i * part:(i + 1) * part] = shards[i]
    for r in range(1, ndp):
        ax_copy(r, d).start()
    for load in loads:
        load.wait()

    def reduce_rows():
        @pl.loop(1, n)
        def _(k):
            peer = lax.rem(t + k, n)
            if_holder(peer, lambda: rs_copy(k, peer, t, peer).start())

        def total():
            mine = pl.ds(pl.multiple_of(t * block, block), block)
            sums[t] = stage[mine, :]

            @pl.loop(1, n)
            def _(k):
                rs_copy(k, t, lax.rem(t - k + n, n), t).wait_recv()

            value = sums[0].astype(jnp.float32)
            for i in range(1, n):
                value = value + sums[i].astype(jnp.float32)
            turned[...] = (a_all[d, mine, :].astype(jnp.float32) + value).astype(jnp.bfloat16)

            @pl.loop(0, n)
            def _(k):
                bc_copy(k, t, lax.rem(t + k, n)).start()

        if_holder(t, total)

    def reduce_done():
        @pl.loop(1, n)
        def _(k):
            peer = lax.rem(t + k, n)
            if_holder(peer, lambda: rs_copy(k, peer, t, peer).wait_send())

        def sent():
            @pl.loop(0, n)
            def _(k):
                bc_copy(k, t, lax.rem(t + k, n)).wait_send()

        if_holder(t, sent)

    def receive_own():
        @pl.loop(0, n)
        def _(k):
            owner = lax.rem(t - k + n, n)

            def take():
                bc_copy(k, owner, t).wait_recv()
                for r in range(1, ndp):
                    fw_copy(r, k, d, owner).start()

            if_holder(owner, take)

    def receive_other(r):
        slot = lax.rem(d - r + ndp, ndp)

        @pl.loop(0, n)
        def _(k):
            owner = lax.rem(t - k + n, n)
            if_holder(owner, lambda: fw_copy(r, k, slot, owner).wait_recv())

    def tiles(size, tile, body):
        @pl.loop(0, size // tile)
        def _(j):
            body(pl.ds(pl.multiple_of(j * tile, tile), tile))

    def forward(x_ref, cols):
        x = x_ref[...]
        gate = dot(x, wg[:, cols]).astype(jnp.bfloat16)
        up = dot(x, wu[:, cols]).astype(jnp.bfloat16)
        return gate, up

    def first_forward(r):
        def body(cols):
            gate, up = forward(a_all.at[r], cols)
            gate_s[r, :, cols] = gate
            up_s[r, :, cols] = up
            hid[r, :, cols] = hidden_of(gate, up)

        tiles(wide, ff_tile, body)

    @pl.when(seg == 0)
    def _():
        first_forward(d)

        def down(cols):
            stage[:, cols] = dot(hid[d], wd[:, cols]).astype(jnp.bfloat16)

        tiles(depth, d_tile, down)
        reduce_rows()
        for r in range(1, ndp):
            slot = lax.rem(d - r + ndp, ndp)
            ax_copy(r, slot).wait_recv()
            first_forward(slot)
        receive_own()

        def backward(r):
            def body(cols):
                d_hidden = dot_nt(b_all[r], wd[cols, :])
                d_gate, d_up = slopes(gate_s[r, :, cols], up_s[r, :, cols], d_hidden)
                dgate[r, :, cols] = d_gate
                dup[r, :, cols] = d_up

            tiles(wide, ff_tile, body)

        backward(d)
        for r in range(1, ndp):
            receive_other(r)
            backward(lax.rem(d - r + ndp, ndp))

    @pl.when(seg == 1)
    def _():
        def early(cols):
            dhid[:, cols] = dot_nt(a_all[d], wd[cols, :])

        tiles(wide, ff_tile, early)
        receive_own()

        def turn(cols):
            gate, up = forward(b_all.at[d], cols)
            d_gate, d_up = slopes(gate, up, dhid[:, cols])
            dgate[d, :, cols] = d_gate
            dup[d, :, cols] = d_up
            hid[d, :, cols] = hidden_of(gate, up)

        tiles(wide, ff_tile, turn)

        def back(cols):
            value = dot_nt(dgate[d], wg[cols, :]) + dot_nt(dup[d], wu[cols, :])
            stage[:, cols] = value.astype(jnp.bfloat16)

        tiles(depth, d_tile, back)
        reduce_rows()
        for r in range(1, ndp):
            slot = lax.rem(d - r + ndp, ndp)
            ax_copy(r, slot).wait_recv()
            receive_other(r)

            def whole(cols):
                d_hidden = dot_nt(a_all[slot], wd[cols, :])
                gate, up = forward(b_all.at[slot], cols)
                d_gate, d_up = slopes(gate, up, d_hidden)
                dgate[slot, :, cols] = d_gate
                dup[slot, :, cols] = d_up
                hid[slot, :, cols] = hidden_of(gate, up)

            tiles(wide, ff_tile, whole)

    saves = [
        pltpu.make_async_copy(source, target, out_sem.at[i])
        for i, (source, target) in enumerate(
            ((a_all, a_out), (b_all, b_out), (hid, h_out), (dgate, dg_out), (dup, du_out))
        )
    ]
    for save in saves:
        save.start()

    @pl.loop(1, n)
    def _(k):
        ag_copy(k, t, lax.rem(t + k, n)).wait_send()

    for r in range(1, ndp):
        ax_copy(r, d).wait_send()
    reduce_done()

    @pl.loop(0, n)
    def _(k):
        owner = lax.rem(t - k + n, n)

        def forwarded():
            for r in range(1, ndp):
                fw_copy(r, k, d, owner).wait_send()

        if_holder(owner, forwarded)

    for save in saves:
        save.wait()


def grads_kernel(where, a, b, hid, dgate, dup, g_gate, g_up, g_down):
    first = where[1] == 0
    acts = jnp.where(first, a[...], b[...])
    cots = jnp.where(first, b[...], a[...])
    g_gate[0] = dot_tn(acts, dgate[...])
    g_up[0] = dot_tn(acts, dup[...])
    g_down[0] = dot_tn(hid[...], cots)


def local(n, ndp, tokens, w_gate, w_up, w_down, cotangent):
    rows, part = tokens.shape
    depth, wide = w_gate.shape[1], w_gate.shape[2]
    block = rows // n
    while block % 16:
        block *= 2
    any_spec = pl.BlockSpec(memory_space=pl.ANY)
    vmem_spec = pl.BlockSpec(memory_space=pltpu.VMEM)
    bf16, f32 = jnp.bfloat16, jnp.float32
    narrow = jax.ShapeDtypeStruct((ndp, rows, depth), bf16)
    broad = jax.ShapeDtypeStruct((ndp, rows, wide), bf16)
    dma = pltpu.SemaphoreType.DMA
    parts = pl.pallas_call(
        functools.partial(relay_kernel, n, ndp, block),
        out_shape=(narrow, narrow, broad, broad, broad),
        in_specs=[vmem_spec, vmem_spec, any_spec, any_spec, any_spec],
        out_specs=(any_spec,) * 5,
        scratch_shapes=[
            pltpu.VMEM((depth, wide), bf16),
            pltpu.VMEM((depth, wide), bf16),
            pltpu.VMEM((wide, depth), bf16),
            pltpu.VMEM((n, rows, part), bf16),
            pltpu.VMEM((ndp, rows, depth), bf16),
            pltpu.VMEM((ndp, rows, depth), bf16),
            pltpu.VMEM((ndp, rows, wide), bf16),
            pltpu.VMEM((ndp, rows, wide), bf16),
            pltpu.VMEM((ndp, rows, wide), bf16),
            pltpu.VMEM((ndp, rows, wide), bf16),
            pltpu.VMEM((ndp, rows, wide), bf16),
            pltpu.VMEM((rows, wide), f32),
            pltpu.VMEM((rows, depth), bf16),
            pltpu.VMEM((n, block, depth), bf16),
            pltpu.VMEM((block, depth), bf16),
            dma((3,)), dma((5,)), dma((n,)), dma((n,)), dma((ndp,)), dma((ndp,)),
            dma((n,)), dma((n,)), dma((n,)), dma((n,)), dma((ndp, n)), dma((ndp, n)),
        ],
        compiler_params=pltpu.CompilerParams(
            collective_id=0, has_side_effects=True, vmem_limit_bytes=VMEM_LIMIT
        ),
    )(tokens, cotangent, w_gate, w_up, w_down)
    count = ndp * rows
    a, b = (value.reshape(count, depth) for value in parts[:2])
    hid, dgate, dup = (value.reshape(count, wide) for value in parts[2:])
    share = depth // ndp
    mine = lax.axis_index("dp")
    if share % 128:
        a = lax.dynamic_slice_in_dim(a, mine * share, share, 1)
        b = lax.dynamic_slice_in_dim(b, mine * share, share, 1)
        mine = jnp.zeros_like(mine)
    where = jnp.stack([mine, lax.axis_index("segment")]).astype(jnp.int32)
    tile = 256 if wide % 256 == 0 else wide
    half = pl.BlockSpec((count, share), lambda j, where: (0, where[0]))
    strip = pl.BlockSpec((count, tile), lambda j, where: (0, j))
    tall = pl.BlockSpec((1, share, tile), lambda j, where: (0, 0, j))
    return pl.pallas_call(
        grads_kernel,
        grid_spec=pltpu.PrefetchScalarGridSpec(
            num_scalar_prefetch=1,
            grid=(wide // tile,),
            in_specs=[half, half, strip, strip, strip],
            out_specs=(tall, tall, pl.BlockSpec((1, tile, share), lambda j, where: (0, j, 0))),
        ),
        out_shape=(
            jax.ShapeDtypeStruct((1, share, wide), f32),
            jax.ShapeDtypeStruct((1, share, wide), f32),
            jax.ShapeDtypeStruct((1, wide, share), f32),
        ),
        compiler_params=pltpu.CompilerParams(vmem_limit_bytes=VMEM_LIMIT),
    )(where, a, b, hid, dgate, dup)


def solution(mesh):
    in_specs = (
        P("dp", "tensor"),
        P("segment", None, "tensor"),
        P("segment", None, "tensor"),
        P("segment", "tensor", None),
        P("dp", "tensor"),
    )
    out_specs = (
        P("segment", "dp", "tensor"),
        P("segment", "dp", "tensor"),
        P("segment", "tensor", "dp"),
    )
    run = functools.partial(local, mesh.shape["tensor"], mesh.shape["dp"])
    return jax.shard_map(run, mesh=mesh, in_specs=in_specs, out_specs=out_specs, check_vma=False)
```

```python
import functools

import jax
import jax.numpy as jnp
from jax import lax
from jax.experimental import pallas as pl
from jax.experimental.pallas import tpu as pltpu
from jax.sharding import PartitionSpec as P

MESH = pl.DeviceIdType.MESH
VMEM_LIMIT = 57 * 1024 * 1024


def tile_of(size):
    for tile in (512, 256, 128):
        if size % tile == 0:
            return tile
    return size


def dot(left, right):
    return jnp.dot(left, right, preferred_element_type=jnp.float32)


def dot_nt(left, right):
    return lax.dot_general(
        left, right, (((1,), (1,)), ((), ())), preferred_element_type=jnp.float32
    )


def hidden_of(gate, up):
    g = gate.astype(jnp.float32)
    return (g * jax.nn.sigmoid(g) * up.astype(jnp.float32)).astype(jnp.bfloat16)


def slopes(gate, up, d_hidden):
    g = gate.astype(jnp.float32)
    u = up.astype(jnp.float32)
    q = jax.nn.sigmoid(g)
    d_gate = (d_hidden * u * q * (1.0 + g * (1.0 - q))).astype(jnp.bfloat16)
    d_up = (d_hidden * g * q).astype(jnp.bfloat16)
    return d_gate, d_up


def relay_kernel(
    n, ndp, block,
    tok, cot, wg_h, wu_h, wd_h,
    at_out, c_out, ht_out, dg_out, du_out,
    wg, wu, wd, shards, a_all, b_all, gate_s, up_s, hid, dgate, dup, dhid, stage, sums, turned,
    acts_t, hid_t, go, w_sem, out_sem, ag_send, ag_recv, ax_send, ax_recv, rs_send, rs_recv, bc_send, bc_recv, fw_send, fw_recv,
):
    seg = lax.axis_index("segment")
    t = lax.axis_index("tensor")
    d = lax.axis_index("dp")
    other = 1 - seg
    rows, depth = a_all.shape[1], a_all.shape[2]
    wide = hid.shape[2]
    part = tok.shape[0]
    share = at_out.shape[0]
    holders = rows // block
    ff_tile, d_tile = tile_of(wide), tile_of(depth)

    loads = [
        pltpu.make_async_copy(source.at[0], target, w_sem.at[i])
        for i, (source, target) in enumerate(((wg_h, wg), (wu_h, wu), (wd_h, wd)))
    ]
    for load in loads:
        load.start()

    def place(s, x, y):
        return {"segment": s, "tensor": x, "dp": y}

    barrier = pltpu.get_barrier_semaphore()

    @pl.loop(0, n)
    def _(k):
        peer = lax.rem(t + k, n)
        pl.semaphore_signal(barrier, inc=1, device_id=place(other, peer, d), device_id_type=MESH)

        @pl.when(k > 0)
        def _():
            pl.semaphore_signal(barrier, inc=1, device_id=place(seg, peer, d), device_id_type=MESH)

    for r in range(1, ndp):
        pl.semaphore_signal(
            barrier, inc=1, device_id=place(seg, t, lax.rem(d + r, ndp)), device_id_type=MESH
        )
    shards[t] = jnp.where(seg == 0, tok[...], cot[...]).T
    pl.semaphore_wait(barrier, 2 * n - 1 + ndp - 1)

    def ag_copy(k, slot, peer):
        return pltpu.make_async_remote_copy(
            src_ref=shards.at[slot], dst_ref=shards.at[slot],
            send_sem=ag_send.at[k], recv_sem=ag_recv.at[k],
            device_id=place(seg, peer, d), device_id_type=MESH,
        )

    def ax_copy(r, slot):
        return pltpu.make_async_remote_copy(
            src_ref=a_all.at[slot], dst_ref=a_all.at[slot],
            send_sem=ax_send.at[r], recv_sem=ax_recv.at[r],
            device_id=place(seg, t, lax.rem(d + r, ndp)), device_id_type=MESH,
        )

    def rs_copy(k, owner, slot, peer):
        return pltpu.make_async_remote_copy(
            src_ref=stage.at[pl.ds(pl.multiple_of(owner * block, block), block)],
            dst_ref=sums.at[slot],
            send_sem=rs_send.at[k], recv_sem=rs_recv.at[k],
            device_id=place(seg, peer, d), device_id_type=MESH,
        )

    def bc_copy(k, owner, peer):
        return pltpu.make_async_remote_copy(
            src_ref=turned,
            dst_ref=b_all.at[d, pl.ds(pl.multiple_of(owner * block, block), block)],
            send_sem=bc_send.at[k], recv_sem=bc_recv.at[k],
            device_id=place(other, peer, d), device_id_type=MESH,
        )

    def fw_copy(r, k, slot, owner):
        here = b_all.at[slot, pl.ds(pl.multiple_of(owner * block, block), block)]
        return pltpu.make_async_remote_copy(
            src_ref=here, dst_ref=here,
            send_sem=fw_send.at[r, k], recv_sem=fw_recv.at[r, k],
            device_id=place(seg, t, lax.rem(d + r, ndp)), device_id_type=MESH,
        )

    def if_holder(index, action):
        if holders == n:
            action()
        else:
            pl.when(index < holders)(action)

    @pl.when(seg == 1)
    def _():
        pl.semaphore_wait(go, 1)

    @pl.loop(1, n)
    def _(k):
        ag_copy(k, t, lax.rem(t + k, n)).start()

    @pl.loop(1, n)
    def _(k):
        ag_copy(k, lax.rem(t - k + n, n), t).wait_recv()

    @pl.when(seg == 0)
    def _():
        pl.semaphore_signal(go, inc=1, device_id=place(1, t, d), device_id_type=MESH)

    for i in range(n):
        a_all[d, :, i * part:(i + 1) * part] = shards[i]
    for r in range(1, ndp):
        ax_copy(r, d).start()
    for load in loads:
        load.wait()

    def reduce_rows():
        @pl.loop(1, n)
        def _(k):
            peer = lax.rem(t + k, n)
            if_holder(peer, lambda: rs_copy(k, peer, t, peer).start())

        def total():
            mine = pl.ds(pl.multiple_of(t * block, block), block)
            sums[t] = stage[mine, :]

            @pl.loop(1, n)
            def _(k):
                rs_copy(k, t, lax.rem(t - k + n, n), t).wait_recv()

            value = sums[0].astype(jnp.float32)
            for i in range(1, n):
                value = value + sums[i].astype(jnp.float32)
            turned[...] = (a_all[d, mine, :].astype(jnp.float32) + value).astype(jnp.bfloat16)

            @pl.loop(0, n)
            def _(k):
                bc_copy(k, t, lax.rem(t + k, n)).start()

        if_holder(t, total)

    def reduce_done():
        @pl.loop(1, n)
        def _(k):
            peer = lax.rem(t + k, n)
            if_holder(peer, lambda: rs_copy(k, peer, t, peer).wait_send())

        def sent():
            @pl.loop(0, n)
            def _(k):
                bc_copy(k, t, lax.rem(t + k, n)).wait_send()

        if_holder(t, sent)

    def receive_own():
        @pl.loop(0, n)
        def _(k):
            owner = lax.rem(t - k + n, n)

            def take():
                bc_copy(k, owner, t).wait_recv()
                for r in range(1, ndp):
                    fw_copy(r, k, d, owner).start()

            if_holder(owner, take)

    def receive_other(r):
        slot = lax.rem(d - r + ndp, ndp)

        @pl.loop(0, n)
        def _(k):
            owner = lax.rem(t - k + n, n)
            if_holder(owner, lambda: fw_copy(r, k, slot, owner).wait_recv())

    def tiles(size, tile, body):
        @pl.loop(0, size // tile)
        def _(j):
            body(pl.ds(pl.multiple_of(j * tile, tile), tile))

    def forward(x_ref, cols):
        x = x_ref[...]
        gate = dot(x, wg[:, cols]).astype(jnp.bfloat16)
        up = dot(x, wu[:, cols]).astype(jnp.bfloat16)
        return gate, up

    def turn_over(r, acts_ref):
        lanes = pl.ds(pl.multiple_of(r * rows, rows), rows)

        def hidden_turned(cols):
            hid_t[cols, lanes] = hid[r, :, cols].T

        def acts_turned(cols):
            acts_t[cols, lanes] = acts_ref[r, :, cols].T

        tiles(wide, ff_tile, hidden_turned)
        tiles(depth, d_tile, acts_turned)

    def save(i, cots_ref):
        narrow = pl.ds(pl.multiple_of(d * share, share), share)
        cots = cots_ref if c_out.shape[2] == depth else cots_ref.at[:, :, narrow]
        source, target = (
            (acts_t.at[narrow], at_out), (hid_t, ht_out), (cots, c_out), (dgate, dg_out), (dup, du_out)
        )[i]
        return pltpu.make_async_copy(source, target, out_sem.at[i])

    def first_forward(r):
        def body(cols):
            gate, up = forward(a_all.at[r], cols)
            gate_s[r, :, cols] = gate
            up_s[r, :, cols] = up
            hid[r, :, cols] = hidden_of(gate, up)

        tiles(wide, ff_tile, body)

    @pl.when(seg == 0)
    def _():
        first_forward(d)

        def down(cols):
            stage[:, cols] = dot(hid[d], wd[:, cols]).astype(jnp.bfloat16)

        tiles(depth, d_tile, down)
        reduce_rows()
        turn_over(d, a_all)
        for r in range(1, ndp):
            slot = lax.rem(d - r + ndp, ndp)
            ax_copy(r, slot).wait_recv()
            first_forward(slot)
            turn_over(slot, a_all)
        save(0, b_all).start()
        save(1, b_all).start()
        receive_own()

        def backward(r):
            def body(cols):
                d_hidden = dot_nt(b_all[r], wd[cols, :])
                d_gate, d_up = slopes(gate_s[r, :, cols], up_s[r, :, cols], d_hidden)
                dgate[r, :, cols] = d_gate
                dup[r, :, cols] = d_up

            tiles(wide, ff_tile, body)

        backward(d)
        for r in range(1, ndp):
            receive_other(r)
            if r == ndp - 1:
                save(2, b_all).start()
            backward(lax.rem(d - r + ndp, ndp))
        save(3, b_all).start()
        save(4, b_all).start()
        for i in range(5):
            save(i, b_all).wait()

    @pl.when(seg == 1)
    def _():
        def early(cols):
            dhid[:, cols] = dot_nt(a_all[d], wd[cols, :])

        tiles(wide, ff_tile, early)
        receive_own()

        def turn(cols):
            gate, up = forward(b_all.at[d], cols)
            d_gate, d_up = slopes(gate, up, dhid[:, cols])
            dgate[d, :, cols] = d_gate
            dup[d, :, cols] = d_up
            hid[d, :, cols] = hidden_of(gate, up)

        tiles(wide, ff_tile, turn)

        def back(cols):
            value = dot_nt(dgate[d], wg[cols, :]) + dot_nt(dup[d], wu[cols, :])
            stage[:, cols] = value.astype(jnp.bfloat16)

        tiles(depth, d_tile, back)
        reduce_rows()
        turn_over(d, b_all)
        for r in range(1, ndp):
            slot = lax.rem(d - r + ndp, ndp)
            ax_copy(r, slot).wait_recv()
            receive_other(r)

            def whole(cols):
                d_hidden = dot_nt(a_all[slot], wd[cols, :])
                gate, up = forward(b_all.at[slot], cols)
                d_gate, d_up = slopes(gate, up, d_hidden)
                dgate[slot, :, cols] = d_gate
                dup[slot, :, cols] = d_up
                hid[slot, :, cols] = hidden_of(gate, up)

            tiles(wide, ff_tile, whole)
            turn_over(slot, b_all)

        for i in range(5):
            save(i, a_all).start()
        for i in range(5):
            save(i, a_all).wait()

    @pl.loop(1, n)
    def _(k):
        ag_copy(k, t, lax.rem(t + k, n)).wait_send()

    for r in range(1, ndp):
        ax_copy(r, d).wait_send()
    reduce_done()

    @pl.loop(0, n)
    def _(k):
        owner = lax.rem(t - k + n, n)

        def forwarded():
            for r in range(1, ndp):
                fw_copy(r, k, d, owner).wait_send()

        if_holder(owner, forwarded)


def grads_kernel(acts_t, hid_t, cots, dgate, dup, g_gate, g_up, g_down):
    g_gate[0] = dot(acts_t[...], dgate[...])
    g_up[0] = dot(acts_t[...], dup[...])
    g_down[0] = dot(hid_t[...], cots[...])


def local(n, ndp, tokens, w_gate, w_up, w_down, cotangent):
    rows, part = tokens.shape
    depth, wide = w_gate.shape[1], w_gate.shape[2]
    block = rows // n
    while block % 16:
        block *= 2
    any_spec = pl.BlockSpec(memory_space=pl.ANY)
    hbm_spec = pl.BlockSpec(memory_space=pltpu.HBM)
    vmem_spec = pl.BlockSpec(memory_space=pltpu.VMEM)
    bf16, f32 = jnp.bfloat16, jnp.float32
    share, count = depth // ndp, ndp * rows
    kept = depth if share % 128 else share
    broad = jax.ShapeDtypeStruct((ndp, rows, wide), bf16)
    dma = pltpu.SemaphoreType.DMA
    parts = pl.pallas_call(
        functools.partial(relay_kernel, n, ndp, block),
        out_shape=(
            jax.ShapeDtypeStruct((share, count), bf16),
            jax.ShapeDtypeStruct((ndp, rows, kept), bf16),
            jax.ShapeDtypeStruct((wide, count), bf16),
            broad,
            broad,
        ),
        in_specs=[vmem_spec, vmem_spec, hbm_spec, hbm_spec, hbm_spec],
        out_specs=(any_spec,) * 5,
        scratch_shapes=[
            pltpu.VMEM((depth, wide), bf16),
            pltpu.VMEM((depth, wide), bf16),
            pltpu.VMEM((wide, depth), bf16),
            pltpu.VMEM((n, rows, part), bf16),
            pltpu.VMEM((ndp, rows, depth), bf16),
            pltpu.VMEM((ndp, rows, depth), bf16),
            pltpu.VMEM((ndp, rows, wide), bf16),
            pltpu.VMEM((ndp, rows, wide), bf16),
            pltpu.VMEM((ndp, rows, wide), bf16),
            pltpu.VMEM((ndp, rows, wide), bf16),
            pltpu.VMEM((ndp, rows, wide), bf16),
            pltpu.VMEM((rows, wide), f32),
            pltpu.VMEM((rows, depth), bf16),
            pltpu.VMEM((n, block, depth), bf16),
            pltpu.VMEM((block, depth), bf16),
            pltpu.VMEM((depth, count), bf16),
            pltpu.VMEM((wide, count), bf16),
            pltpu.SemaphoreType.REGULAR,
            dma((3,)), dma((5,)), dma((n,)), dma((n,)), dma((ndp,)), dma((ndp,)),
            dma((n,)), dma((n,)), dma((n,)), dma((n,)), dma((ndp, n)), dma((ndp, n)),
        ],
        compiler_params=pltpu.CompilerParams(
            collective_id=0, has_side_effects=True, vmem_limit_bytes=VMEM_LIMIT
        ),
    )(tokens.T, cotangent.T, w_gate, w_up, w_down)
    acts_t, cots, hid_t, dgate, dup = parts
    if kept != share:
        cots = lax.dynamic_slice_in_dim(cots, lax.axis_index("dp") * share, share, 2)
    cots = cots.reshape(count, share)
    dgate, dup = (value.reshape(count, wide) for value in (dgate, dup))
    tile = 256 if wide % 256 == 0 else wide
    strip = pl.BlockSpec((count, tile), lambda j: (0, j))
    tall = pl.BlockSpec((1, share, tile), lambda j: (0, 0, j))
    return pl.pallas_call(
        grads_kernel,
        grid=(wide // tile,),
        in_specs=[
            pl.BlockSpec((share, count), lambda j: (0, 0)),
            pl.BlockSpec((tile, count), lambda j: (j, 0)),
            pl.BlockSpec((count, share), lambda j: (0, 0)),
            strip,
            strip,
        ],
        out_specs=(tall, tall, pl.BlockSpec((1, tile, share), lambda j: (0, j, 0))),
        out_shape=(
            jax.ShapeDtypeStruct((1, share, wide), f32),
            jax.ShapeDtypeStruct((1, share, wide), f32),
            jax.ShapeDtypeStruct((1, wide, share), f32),
        ),
        compiler_params=pltpu.CompilerParams(vmem_limit_bytes=VMEM_LIMIT),
    )(acts_t, hid_t, cots, dgate, dup)


def solution(mesh):
    in_specs = (
        P("dp", "tensor"),
        P("segment", None, "tensor"),
        P("segment", None, "tensor"),
        P("segment", "tensor", None),
        P("dp", "tensor"),
    )
    out_specs = (
        P("segment", "dp", "tensor"),
        P("segment", "dp", "tensor"),
        P("segment", "tensor", "dp"),
    )
    run = functools.partial(local, mesh.shape["tensor"], mesh.shape["dp"])
    return jax.shard_map(run, mesh=mesh, in_specs=in_specs, out_specs=out_specs, check_vma=False)
```

```python
import functools

import jax
import jax.numpy as jnp
from jax import lax
from jax.experimental import pallas as pl
from jax.experimental.pallas import tpu as pltpu
from jax.sharding import PartitionSpec as P

MESH = pl.DeviceIdType.MESH
VMEM_LIMIT = 57 * 1024 * 1024


def tile_of(size):
    for tile in (512, 256, 128):
        if size % tile == 0:
            return tile
    return size


def dot(left, right):
    return jnp.dot(left, right, preferred_element_type=jnp.float32)


def dot_nt(left, right):
    return lax.dot_general(
        left, right, (((1,), (1,)), ((), ())), preferred_element_type=jnp.float32
    )


def hidden_of(gate, up):
    g = gate.astype(jnp.float32)
    return (g * jax.nn.sigmoid(g) * up.astype(jnp.float32)).astype(jnp.bfloat16)


def slopes(gate, up, d_hidden):
    g = gate.astype(jnp.float32)
    u = up.astype(jnp.float32)
    q = jax.nn.sigmoid(g)
    d_gate = (d_hidden * u * q * (1.0 + g * (1.0 - q))).astype(jnp.bfloat16)
    d_up = (d_hidden * g * q).astype(jnp.bfloat16)
    return d_gate, d_up


def relay_kernel(
    n, ndp, block,
    tok, cot, wg_h, wu_h, wd_h,
    at_out, c_out, ht_out, dg_out, du_out,
    wg, wu, wd, shards, a_all, b_all, gate_s, up_s, hid, dgate, dup, dhid, stage, sums, turned,
    acts_t, hid_t, go, w_sem, out_sem, ag_send, ag_recv, ax_send, ax_recv, rs_send, rs_recv, bc_send, bc_recv, fw_send, fw_recv,
):
    seg = lax.axis_index("segment")
    t = lax.axis_index("tensor")
    d = lax.axis_index("dp")
    other = 1 - seg
    rows, depth = a_all.shape[1], a_all.shape[2]
    wide = hid.shape[2]
    part = tok.shape[0]
    share = at_out.shape[0]
    holders = rows // block
    ff_tile, d_tile = tile_of(wide), tile_of(depth)

    loads = [
        pltpu.make_async_copy(source.at[0], target, w_sem.at[i])
        for i, (source, target) in enumerate(((wg_h, wg), (wu_h, wu), (wd_h, wd)))
    ]
    for load in loads:
        load.start()

    def place(s, x, y):
        return {"segment": s, "tensor": x, "dp": y}

    barrier = pltpu.get_barrier_semaphore()

    @pl.loop(0, n)
    def _(k):
        peer = lax.rem(t + k, n)
        pl.semaphore_signal(barrier, inc=1, device_id=place(other, peer, d), device_id_type=MESH)

        @pl.when(k > 0)
        def _():
            pl.semaphore_signal(barrier, inc=1, device_id=place(seg, peer, d), device_id_type=MESH)

    for r in range(1, ndp):
        pl.semaphore_signal(
            barrier, inc=1, device_id=place(seg, t, lax.rem(d + r, ndp)), device_id_type=MESH
        )
    shards[t] = jnp.where(seg == 0, tok[...], cot[...]).T
    pl.semaphore_wait(barrier, 2 * n - 1 + ndp - 1)

    def ag_copy(k, slot, peer):
        return pltpu.make_async_remote_copy(
            src_ref=shards.at[slot], dst_ref=shards.at[slot],
            send_sem=ag_send.at[k], recv_sem=ag_recv.at[k],
            device_id=place(seg, peer, d), device_id_type=MESH,
        )

    def ax_copy(r, slot):
        return pltpu.make_async_remote_copy(
            src_ref=a_all.at[slot], dst_ref=a_all.at[slot],
            send_sem=ax_send.at[r], recv_sem=ax_recv.at[r],
            device_id=place(seg, t, lax.rem(d + r, ndp)), device_id_type=MESH,
        )

    def columns(c):
        return pl.ds(pl.multiple_of(c * d_tile, d_tile), d_tile)

    def rs_copy(k, c, owner, slot, peer):
        return pltpu.make_async_remote_copy(
            src_ref=stage.at[pl.ds(pl.multiple_of(owner * block, block), block), columns(c)],
            dst_ref=sums.at[slot, :, columns(c)],
            send_sem=rs_send.at[k, c], recv_sem=rs_recv.at[k, c],
            device_id=place(seg, peer, d), device_id_type=MESH,
        )

    def bc_copy(k, c, owner, peer):
        return pltpu.make_async_remote_copy(
            src_ref=turned.at[:, columns(c)],
            dst_ref=b_all.at[d, pl.ds(pl.multiple_of(owner * block, block), block), columns(c)],
            send_sem=bc_send.at[k, c], recv_sem=bc_recv.at[k, c],
            device_id=place(other, peer, d), device_id_type=MESH,
        )

    def fw_copy(r, k, slot, owner):
        here = b_all.at[slot, pl.ds(pl.multiple_of(owner * block, block), block)]
        return pltpu.make_async_remote_copy(
            src_ref=here, dst_ref=here,
            send_sem=fw_send.at[r, k], recv_sem=fw_recv.at[r, k],
            device_id=place(seg, t, lax.rem(d + r, ndp)), device_id_type=MESH,
        )

    def if_holder(index, action):
        if holders == n:
            action()
        else:
            pl.when(index < holders)(action)

    @pl.when(seg == 1)
    def _():
        pl.semaphore_wait(go, 1)

    @pl.loop(1, n)
    def _(k):
        ag_copy(k, t, lax.rem(t + k, n)).start()

    @pl.loop(1, n)
    def _(k):
        ag_copy(k, lax.rem(t - k + n, n), t).wait_recv()

    @pl.when(seg == 0)
    def _():
        pl.semaphore_signal(go, inc=1, device_id=place(1, t, d), device_id_type=MESH)

    for i in range(n):
        a_all[d, :, i * part:(i + 1) * part] = shards[i]
    for r in range(1, ndp):
        ax_copy(r, d).start()
    for load in loads:
        load.wait()

    chunks = depth // d_tile

    def reduce_rows(product):
        @pl.loop(0, chunks)
        def _(c):
            stage[:, columns(c)] = product(columns(c)).astype(jnp.bfloat16)

            @pl.loop(1, n)
            def _(k):
                peer = lax.rem(t + k, n)
                if_holder(peer, lambda: rs_copy(k, c, peer, t, peer).start())

        def total():
            mine = pl.ds(pl.multiple_of(t * block, block), block)
            sums[t] = stage[mine, :]

            @pl.loop(0, chunks)
            def _(c):
                @pl.loop(1, n)
                def _(k):
                    rs_copy(k, c, t, lax.rem(t - k + n, n), t).wait_recv()

                cols = columns(c)
                value = sums[0, :, cols].astype(jnp.float32)
                for i in range(1, n):
                    value = value + sums[i, :, cols].astype(jnp.float32)
                value = a_all[d, mine, cols].astype(jnp.float32) + value
                turned[:, cols] = value.astype(jnp.bfloat16)

                @pl.loop(0, n)
                def _(k):
                    bc_copy(k, c, t, lax.rem(t + k, n)).start()

        if_holder(t, total)

    def reduce_done():
        @pl.loop(0, chunks)
        def _(c):
            @pl.loop(1, n)
            def _(k):
                peer = lax.rem(t + k, n)
                if_holder(peer, lambda: rs_copy(k, c, peer, t, peer).wait_send())

        def sent():
            @pl.loop(0, chunks)
            def _(c):
                @pl.loop(0, n)
                def _(k):
                    bc_copy(k, c, t, lax.rem(t + k, n)).wait_send()

        if_holder(t, sent)

    def receive_own():
        @pl.loop(0, n)
        def _(k):
            owner = lax.rem(t - k + n, n)

            def take():
                @pl.loop(0, chunks)
                def _(c):
                    bc_copy(k, c, owner, t).wait_recv()

                for r in range(1, ndp):
                    fw_copy(r, k, d, owner).start()

            if_holder(owner, take)

    def receive_other(r):
        slot = lax.rem(d - r + ndp, ndp)

        @pl.loop(0, n)
        def _(k):
            owner = lax.rem(t - k + n, n)
            if_holder(owner, lambda: fw_copy(r, k, slot, owner).wait_recv())

    def tiles(size, tile, body):
        @pl.loop(0, size // tile)
        def _(j):
            body(pl.ds(pl.multiple_of(j * tile, tile), tile))

    def forward(x_ref, cols):
        x = x_ref[...]
        gate = dot(x, wg[:, cols]).astype(jnp.bfloat16)
        up = dot(x, wu[:, cols]).astype(jnp.bfloat16)
        return gate, up

    def turn_over(r, acts_ref):
        lanes = pl.ds(pl.multiple_of(r * rows, rows), rows)

        def hidden_turned(cols):
            hid_t[cols, lanes] = hid[r, :, cols].T

        def acts_turned(cols):
            acts_t[cols, lanes] = acts_ref[r, :, cols].T

        tiles(wide, ff_tile, hidden_turned)
        tiles(depth, d_tile, acts_turned)

    def save(i, cots_ref):
        narrow = pl.ds(pl.multiple_of(d * share, share), share)
        cots = cots_ref if c_out.shape[2] == depth else cots_ref.at[:, :, narrow]
        source, target = (
            (acts_t.at[narrow], at_out), (hid_t, ht_out), (cots, c_out), (dgate, dg_out), (dup, du_out)
        )[i]
        return pltpu.make_async_copy(source, target, out_sem.at[i])

    def first_forward(r):
        def body(cols):
            gate, up = forward(a_all.at[r], cols)
            gate_s[r, :, cols] = gate
            up_s[r, :, cols] = up
            hid[r, :, cols] = hidden_of(gate, up)

        tiles(wide, ff_tile, body)

    @pl.when(seg == 0)
    def _():
        first_forward(d)

        reduce_rows(lambda cols: dot(hid[d], wd[:, cols]))
        turn_over(d, a_all)
        for r in range(1, ndp):
            slot = lax.rem(d - r + ndp, ndp)
            ax_copy(r, slot).wait_recv()
            first_forward(slot)
            turn_over(slot, a_all)
        save(0, b_all).start()
        save(1, b_all).start()
        receive_own()

        def backward(r):
            def body(cols):
                d_hidden = dot_nt(b_all[r], wd[cols, :])
                d_gate, d_up = slopes(gate_s[r, :, cols], up_s[r, :, cols], d_hidden)
                dgate[r, :, cols] = d_gate
                dup[r, :, cols] = d_up

            tiles(wide, ff_tile, body)

        backward(d)
        for r in range(1, ndp):
            receive_other(r)
            if r == ndp - 1:
                save(2, b_all).start()
            backward(lax.rem(d - r + ndp, ndp))
        save(3, b_all).start()
        save(4, b_all).start()
        for i in range(5):
            save(i, b_all).wait()

    @pl.when(seg == 1)
    def _():
        def early(cols):
            dhid[:, cols] = dot_nt(a_all[d], wd[cols, :])

        tiles(wide, ff_tile, early)
        receive_own()

        def turn(cols):
            gate, up = forward(b_all.at[d], cols)
            d_gate, d_up = slopes(gate, up, dhid[:, cols])
            dgate[d, :, cols] = d_gate
            dup[d, :, cols] = d_up
            hid[d, :, cols] = hidden_of(gate, up)

        tiles(wide, ff_tile, turn)

        reduce_rows(lambda cols: dot_nt(dgate[d], wg[cols, :]) + dot_nt(dup[d], wu[cols, :]))
        turn_over(d, b_all)
        for r in range(1, ndp):
            slot = lax.rem(d - r + ndp, ndp)
            ax_copy(r, slot).wait_recv()
            receive_other(r)

            def whole(cols):
                d_hidden = dot_nt(a_all[slot], wd[cols, :])
                gate, up = forward(b_all.at[slot], cols)
                d_gate, d_up = slopes(gate, up, d_hidden)
                dgate[slot, :, cols] = d_gate
                dup[slot, :, cols] = d_up
                hid[slot, :, cols] = hidden_of(gate, up)

            tiles(wide, ff_tile, whole)
            turn_over(slot, b_all)

        for i in range(5):
            save(i, a_all).start()
        for i in range(5):
            save(i, a_all).wait()

    @pl.loop(1, n)
    def _(k):
        ag_copy(k, t, lax.rem(t + k, n)).wait_send()

    for r in range(1, ndp):
        ax_copy(r, d).wait_send()
    reduce_done()

    @pl.loop(0, n)
    def _(k):
        owner = lax.rem(t - k + n, n)

        def forwarded():
            for r in range(1, ndp):
                fw_copy(r, k, d, owner).wait_send()

        if_holder(owner, forwarded)


def grads_kernel(acts_t, hid_t, cots, dgate, dup, g_gate, g_up, g_down):
    g_gate[0] = dot(acts_t[...], dgate[...])
    g_up[0] = dot(acts_t[...], dup[...])
    g_down[0] = dot(hid_t[...], cots[...])


def local(n, ndp, tokens, w_gate, w_up, w_down, cotangent):
    rows, part = tokens.shape
    depth, wide = w_gate.shape[1], w_gate.shape[2]
    block = rows // n
    while block % 16:
        block *= 2
    any_spec = pl.BlockSpec(memory_space=pl.ANY)
    hbm_spec = pl.BlockSpec(memory_space=pltpu.HBM)
    vmem_spec = pl.BlockSpec(memory_space=pltpu.VMEM)
    bf16, f32 = jnp.bfloat16, jnp.float32
    share, count = depth // ndp, ndp * rows
    kept = depth if share % 128 else share
    broad = jax.ShapeDtypeStruct((ndp, rows, wide), bf16)
    dma = pltpu.SemaphoreType.DMA
    chunks = depth // tile_of(depth)
    parts = pl.pallas_call(
        functools.partial(relay_kernel, n, ndp, block),
        out_shape=(
            jax.ShapeDtypeStruct((share, count), bf16),
            jax.ShapeDtypeStruct((ndp, rows, kept), bf16),
            jax.ShapeDtypeStruct((wide, count), bf16),
            broad,
            broad,
        ),
        in_specs=[vmem_spec, vmem_spec, hbm_spec, hbm_spec, hbm_spec],
        out_specs=(any_spec,) * 5,
        scratch_shapes=[
            pltpu.VMEM((depth, wide), bf16),
            pltpu.VMEM((depth, wide), bf16),
            pltpu.VMEM((wide, depth), bf16),
            pltpu.VMEM((n, rows, part), bf16),
            pltpu.VMEM((ndp, rows, depth), bf16),
            pltpu.VMEM((ndp, rows, depth), bf16),
            pltpu.VMEM((ndp, rows, wide), bf16),
            pltpu.VMEM((ndp, rows, wide), bf16),
            pltpu.VMEM((ndp, rows, wide), bf16),
            pltpu.VMEM((ndp, rows, wide), bf16),
            pltpu.VMEM((ndp, rows, wide), bf16),
            pltpu.VMEM((rows, wide), f32),
            pltpu.VMEM((rows, depth), bf16),
            pltpu.VMEM((n, block, depth), bf16),
            pltpu.VMEM((block, depth), bf16),
            pltpu.VMEM((depth, count), bf16),
            pltpu.VMEM((wide, count), bf16),
            pltpu.SemaphoreType.REGULAR,
            dma((3,)), dma((5,)), dma((n,)), dma((n,)), dma((ndp,)), dma((ndp,)),
            dma((n, chunks)), dma((n, chunks)), dma((n, chunks)), dma((n, chunks)), dma((ndp, n)), dma((ndp, n)),
        ],
        compiler_params=pltpu.CompilerParams(
            collective_id=0, has_side_effects=True, vmem_limit_bytes=VMEM_LIMIT
        ),
    )(tokens.T, cotangent.T, w_gate, w_up, w_down)
    acts_t, cots, hid_t, dgate, dup = parts
    if kept != share:
        cots = lax.dynamic_slice_in_dim(cots, lax.axis_index("dp") * share, share, 2)
    cots = cots.reshape(count, share)
    dgate, dup = (value.reshape(count, wide) for value in (dgate, dup))
    tile = tile_of(wide)
    strip = pl.BlockSpec((count, tile), lambda j: (0, j))
    tall = pl.BlockSpec((1, share, tile), lambda j: (0, 0, j))
    return pl.pallas_call(
        grads_kernel,
        grid=(wide // tile,),
        in_specs=[
            pl.BlockSpec((share, count), lambda j: (0, 0)),
            pl.BlockSpec((tile, count), lambda j: (j, 0)),
            pl.BlockSpec((count, share), lambda j: (0, 0)),
            strip,
            strip,
        ],
        out_specs=(tall, tall, pl.BlockSpec((1, tile, share), lambda j: (0, j, 0))),
        out_shape=(
            jax.ShapeDtypeStruct((1, share, wide), f32),
            jax.ShapeDtypeStruct((1, share, wide), f32),
            jax.ShapeDtypeStruct((1, wide, share), f32),
        ),
        compiler_params=pltpu.CompilerParams(vmem_limit_bytes=VMEM_LIMIT),
    )(acts_t, hid_t, cots, dgate, dup)


def solution(mesh):
    in_specs = (
        P("dp", "tensor"),
        P("segment", None, "tensor"),
        P("segment", None, "tensor"),
        P("segment", "tensor", None),
        P("dp", "tensor"),
    )
    out_specs = (
        P("segment", "dp", "tensor"),
        P("segment", "dp", "tensor"),
        P("segment", "tensor", "dp"),
    )
    run = functools.partial(local, mesh.shape["tensor"], mesh.shape["dp"])
    return jax.shard_map(run, mesh=mesh, in_specs=in_specs, out_specs=out_specs, check_vma=False)
```

```python
import functools

import jax
import jax.numpy as jnp
from jax import lax
from jax.experimental import pallas as pl
from jax.experimental.pallas import tpu as pltpu
from jax.sharding import PartitionSpec as P

MESH = pl.DeviceIdType.MESH
VMEM_LIMIT = 57 * 1024 * 1024


def tile_of(size):
    for tile in (512, 256, 128):
        if size % tile == 0:
            return tile
    return size


def dot(left, right):
    return jnp.dot(left, right, preferred_element_type=jnp.float32)


def dot_nt(left, right):
    return lax.dot_general(
        left, right, (((1,), (1,)), ((), ())), preferred_element_type=jnp.float32
    )


def hidden_of(gate, up):
    g = gate.astype(jnp.float32)
    return (g * jax.nn.sigmoid(g) * up.astype(jnp.float32)).astype(jnp.bfloat16)


def slopes(gate, up, d_hidden):
    g = gate.astype(jnp.float32)
    u = up.astype(jnp.float32)
    q = jax.nn.sigmoid(g)
    d_gate = (d_hidden * u * q * (1.0 + g * (1.0 - q))).astype(jnp.bfloat16)
    d_up = (d_hidden * g * q).astype(jnp.bfloat16)
    return d_gate, d_up


def relay_kernel(
    n, ndp, block,
    tok, cot, wg_h, wu_h, wd_h,
    at_out, c_out, ht_out, dg_out, du_out,
    wg, wu, wd, shards, a_all, b_all, gate_s, up_s, hid, dgate, dup, dhid, stage, sums, turned,
    acts_t, hid_t, go, w_sem, out_sem, ag_send, ag_recv, ax_send, ax_recv, rs_send, rs_recv, bc_send, bc_recv, fw_send, fw_recv,
):
    seg = lax.axis_index("segment")
    t = lax.axis_index("tensor")
    d = lax.axis_index("dp")
    other = 1 - seg
    rows, depth = a_all.shape[1], a_all.shape[2]
    wide = hid.shape[2]
    part = tok.shape[0]
    share = at_out.shape[0]
    holders = rows // block
    ff_tile, d_tile = tile_of(wide), tile_of(depth)

    loads = [
        pltpu.make_async_copy(source.at[0], target, w_sem.at[i])
        for i, (source, target) in enumerate(((wg_h, wg), (wu_h, wu), (wd_h, wd)))
    ]
    for load in loads:
        load.start()

    def place(s, x, y):
        return {"segment": s, "tensor": x, "dp": y}

    barrier = pltpu.get_barrier_semaphore()

    @pl.loop(0, n)
    def _(k):
        peer = lax.rem(t + k, n)
        pl.semaphore_signal(barrier, inc=1, device_id=place(other, peer, d), device_id_type=MESH)

        @pl.when(k > 0)
        def _():
            pl.semaphore_signal(barrier, inc=1, device_id=place(seg, peer, d), device_id_type=MESH)

    for r in range(1, ndp):
        pl.semaphore_signal(
            barrier, inc=1, device_id=place(seg, t, lax.rem(d + r, ndp)), device_id_type=MESH
        )
    shards[t] = jnp.where(seg == 0, tok[...], cot[...]).T
    pl.semaphore_wait(barrier, 2 * n - 1 + ndp - 1)

    def ag_copy(k, slot, peer):
        return pltpu.make_async_remote_copy(
            src_ref=shards.at[slot], dst_ref=shards.at[slot],
            send_sem=ag_send.at[k], recv_sem=ag_recv.at[k],
            device_id=place(seg, peer, d), device_id_type=MESH,
        )

    def ax_copy(r, slot):
        return pltpu.make_async_remote_copy(
            src_ref=a_all.at[slot], dst_ref=a_all.at[slot],
            send_sem=ax_send.at[r], recv_sem=ax_recv.at[r],
            device_id=place(seg, t, lax.rem(d + r, ndp)), device_id_type=MESH,
        )

    def columns(c):
        return pl.ds(pl.multiple_of(c * d_tile, d_tile), d_tile)

    def rs_copy(k, c, owner, slot, peer):
        return pltpu.make_async_remote_copy(
            src_ref=stage.at[pl.ds(pl.multiple_of(owner * block, block), block), columns(c)],
            dst_ref=sums.at[slot, :, columns(c)],
            send_sem=rs_send.at[k, c], recv_sem=rs_recv.at[k, c],
            device_id=place(seg, peer, d), device_id_type=MESH,
        )

    def bc_copy(k, c, owner, peer):
        return pltpu.make_async_remote_copy(
            src_ref=turned.at[:, columns(c)],
            dst_ref=b_all.at[d, pl.ds(pl.multiple_of(owner * block, block), block), columns(c)],
            send_sem=bc_send.at[k, c], recv_sem=bc_recv.at[k, c],
            device_id=place(other, peer, d), device_id_type=MESH,
        )

    def fw_copy(r, k, slot, owner):
        here = b_all.at[slot, pl.ds(pl.multiple_of(owner * block, block), block)]
        return pltpu.make_async_remote_copy(
            src_ref=here, dst_ref=here,
            send_sem=fw_send.at[r, k], recv_sem=fw_recv.at[r, k],
            device_id=place(seg, t, lax.rem(d + r, ndp)), device_id_type=MESH,
        )

    def if_holder(index, action):
        if holders == n:
            action()
        else:
            pl.when(index < holders)(action)

    @pl.when(seg == 1)
    def _():
        pl.semaphore_wait(go, 1)

    @pl.loop(1, n, unroll=True)
    def _(k):
        ag_copy(k, t, lax.rem(t + k, n)).start()

    @pl.loop(1, n)
    def _(k):
        ag_copy(k, lax.rem(t - k + n, n), t).wait_recv()

    @pl.when(seg == 0)
    def _():
        pl.semaphore_signal(go, inc=1, device_id=place(1, t, d), device_id_type=MESH)

    for i in range(n):
        a_all[d, :, i * part:(i + 1) * part] = shards[i]
    for r in range(1, ndp):
        ax_copy(r, d).start()
    for load in loads:
        load.wait()

    chunks = depth // d_tile

    def reduce_rows(product):
        @pl.loop(0, chunks)
        def _(c):
            stage[:, columns(c)] = product(columns(c)).astype(jnp.bfloat16)

            @pl.loop(1, n)
            def _(k):
                peer = lax.rem(t + k, n)
                if_holder(peer, lambda: rs_copy(k, c, peer, t, peer).start())

        def total():
            mine = pl.ds(pl.multiple_of(t * block, block), block)
            sums[t] = stage[mine, :]

            @pl.loop(0, chunks)
            def _(c):
                @pl.loop(1, n)
                def _(k):
                    rs_copy(k, c, t, lax.rem(t - k + n, n), t).wait_recv()

                cols = columns(c)
                value = sums[0, :, cols].astype(jnp.float32)
                for i in range(1, n):
                    value = value + sums[i, :, cols].astype(jnp.float32)
                value = a_all[d, mine, cols].astype(jnp.float32) + value
                turned[:, cols] = value.astype(jnp.bfloat16)

                @pl.loop(0, n, unroll=True)
                def _(k):
                    bc_copy(k, c, t, lax.rem(t + k, n)).start()

        if_holder(t, total)

    def reduce_done():
        @pl.loop(0, chunks)
        def _(c):
            @pl.loop(1, n)
            def _(k):
                peer = lax.rem(t + k, n)
                if_holder(peer, lambda: rs_copy(k, c, peer, t, peer).wait_send())

        def sent():
            @pl.loop(0, chunks)
            def _(c):
                @pl.loop(0, n)
                def _(k):
                    bc_copy(k, c, t, lax.rem(t + k, n)).wait_send()

        if_holder(t, sent)

    def receive_own():
        @pl.loop(0, n)
        def _(k):
            owner = lax.rem(t - k + n, n)

            def take():
                @pl.loop(0, chunks)
                def _(c):
                    bc_copy(k, c, owner, t).wait_recv()

                for r in range(1, ndp):
                    fw_copy(r, k, d, owner).start()

            if_holder(owner, take)

    def receive_other(r):
        slot = lax.rem(d - r + ndp, ndp)

        @pl.loop(0, n)
        def _(k):
            owner = lax.rem(t - k + n, n)
            if_holder(owner, lambda: fw_copy(r, k, slot, owner).wait_recv())

    def tiles(size, tile, body):
        @pl.loop(0, size // tile)
        def _(j):
            body(pl.ds(pl.multiple_of(j * tile, tile), tile))

    def forward(x_ref, cols):
        x = x_ref[...]
        gate = dot(x, wg[:, cols]).astype(jnp.bfloat16)
        up = dot(x, wu[:, cols]).astype(jnp.bfloat16)
        return gate, up

    def turn_over(r, acts_ref):
        lanes = pl.ds(pl.multiple_of(r * rows, rows), rows)

        def hidden_turned(cols):
            hid_t[cols, lanes] = hid[r, :, cols].T

        def acts_turned(cols):
            acts_t[cols, lanes] = acts_ref[r, :, cols].T

        tiles(wide, ff_tile, hidden_turned)
        tiles(depth, d_tile, acts_turned)

    def save(i, cots_ref):
        narrow = pl.ds(pl.multiple_of(d * share, share), share)
        cots = cots_ref if c_out.shape[2] == depth else cots_ref.at[:, :, narrow]
        source, target = (
            (acts_t.at[narrow], at_out), (hid_t, ht_out), (cots, c_out), (dgate, dg_out), (dup, du_out)
        )[i]
        return pltpu.make_async_copy(source, target, out_sem.at[i])

    def first_forward(r):
        def body(cols):
            gate, up = forward(a_all.at[r], cols)
            gate_s[r, :, cols] = gate
            up_s[r, :, cols] = up
            hid[r, :, cols] = hidden_of(gate, up)

        tiles(wide, ff_tile, body)

    def early_sent():
        @pl.loop(1, n)
        def _(k):
            ag_copy(k, t, lax.rem(t + k, n)).wait_send()

        for r in range(1, ndp):
            ax_copy(r, d).wait_send()
        reduce_done()

    def forwards_sent():
        @pl.loop(0, n)
        def _(k):
            owner = lax.rem(t - k + n, n)

            def forwarded():
                for r in range(1, ndp):
                    fw_copy(r, k, d, owner).wait_send()

            if_holder(owner, forwarded)

    @pl.when(seg == 0)
    def _():
        first_forward(d)

        reduce_rows(lambda cols: dot(hid[d], wd[:, cols]))
        turn_over(d, a_all)
        for r in range(1, ndp):
            slot = lax.rem(d - r + ndp, ndp)
            ax_copy(r, slot).wait_recv()
            first_forward(slot)
            turn_over(slot, a_all)
        save(0, b_all).start()
        save(1, b_all).start()
        early_sent()
        receive_own()

        def backward(r):
            def body(cols):
                d_hidden = dot_nt(b_all[r], wd[cols, :])
                d_gate, d_up = slopes(gate_s[r, :, cols], up_s[r, :, cols], d_hidden)
                dgate[r, :, cols] = d_gate
                dup[r, :, cols] = d_up

            tiles(wide, ff_tile, body)

        backward(d)
        for r in range(1, ndp):
            receive_other(r)
            if r == ndp - 1:
                save(2, b_all).start()
            backward(lax.rem(d - r + ndp, ndp))
        save(3, b_all).start()
        save(4, b_all).start()
        forwards_sent()
        for i in range(5):
            save(i, b_all).wait()

    @pl.when(seg == 1)
    def _():
        def early(cols):
            dhid[:, cols] = dot_nt(a_all[d], wd[cols, :])

        tiles(wide, ff_tile, early)
        receive_own()

        def turn(cols):
            gate, up = forward(b_all.at[d], cols)
            d_gate, d_up = slopes(gate, up, dhid[:, cols])
            dgate[d, :, cols] = d_gate
            dup[d, :, cols] = d_up
            hid[d, :, cols] = hidden_of(gate, up)

        tiles(wide, ff_tile, turn)

        reduce_rows(lambda cols: dot_nt(dgate[d], wg[cols, :]) + dot_nt(dup[d], wu[cols, :]))
        turn_over(d, b_all)
        for r in range(1, ndp):
            slot = lax.rem(d - r + ndp, ndp)
            ax_copy(r, slot).wait_recv()
            receive_other(r)

            def whole(cols):
                d_hidden = dot_nt(a_all[slot], wd[cols, :])
                gate, up = forward(b_all.at[slot], cols)
                d_gate, d_up = slopes(gate, up, d_hidden)
                dgate[slot, :, cols] = d_gate
                dup[slot, :, cols] = d_up
                hid[slot, :, cols] = hidden_of(gate, up)

            tiles(wide, ff_tile, whole)
            turn_over(slot, b_all)

        for i in range(5):
            save(i, a_all).start()
        early_sent()
        forwards_sent()
        for i in range(5):
            save(i, a_all).wait()


def grads_kernel(acts_t, hid_t, cots, dgate, dup, g_gate, g_up, g_down):
    g_gate[0] = dot(acts_t[...], dgate[...])
    g_up[0] = dot(acts_t[...], dup[...])
    g_down[0] = dot(hid_t[...], cots[...])


def local(n, ndp, tokens, w_gate, w_up, w_down, cotangent):
    rows, part = tokens.shape
    depth, wide = w_gate.shape[1], w_gate.shape[2]
    block = rows // n
    while block % 16:
        block *= 2
    any_spec = pl.BlockSpec(memory_space=pl.ANY)
    hbm_spec = pl.BlockSpec(memory_space=pltpu.HBM)
    vmem_spec = pl.BlockSpec(memory_space=pltpu.VMEM)
    bf16, f32 = jnp.bfloat16, jnp.float32
    share, count = depth // ndp, ndp * rows
    kept = depth if share % 128 else share
    broad = jax.ShapeDtypeStruct((ndp, rows, wide), bf16)
    dma = pltpu.SemaphoreType.DMA
    chunks = depth // tile_of(depth)
    parts = pl.pallas_call(
        functools.partial(relay_kernel, n, ndp, block),
        out_shape=(
            jax.ShapeDtypeStruct((share, count), bf16),
            jax.ShapeDtypeStruct((ndp, rows, kept), bf16),
            jax.ShapeDtypeStruct((wide, count), bf16),
            broad,
            broad,
        ),
        in_specs=[vmem_spec, vmem_spec, hbm_spec, hbm_spec, hbm_spec],
        out_specs=(any_spec,) * 5,
        scratch_shapes=[
            pltpu.VMEM((depth, wide), bf16),
            pltpu.VMEM((depth, wide), bf16),
            pltpu.VMEM((wide, depth), bf16),
            pltpu.VMEM((n, rows, part), bf16),
            pltpu.VMEM((ndp, rows, depth), bf16),
            pltpu.VMEM((ndp, rows, depth), bf16),
            pltpu.VMEM((ndp, rows, wide), bf16),
            pltpu.VMEM((ndp, rows, wide), bf16),
            pltpu.VMEM((ndp, rows, wide), bf16),
            pltpu.VMEM((ndp, rows, wide), bf16),
            pltpu.VMEM((ndp, rows, wide), bf16),
            pltpu.VMEM((rows, wide), f32),
            pltpu.VMEM((rows, depth), bf16),
            pltpu.VMEM((n, block, depth), bf16),
            pltpu.VMEM((block, depth), bf16),
            pltpu.VMEM((depth, count), bf16),
            pltpu.VMEM((wide, count), bf16),
            pltpu.SemaphoreType.REGULAR,
            dma((3,)), dma((5,)), dma((n,)), dma((n,)), dma((ndp,)), dma((ndp,)),
            dma((n, chunks)), dma((n, chunks)), dma((n, chunks)), dma((n, chunks)), dma((ndp, n)), dma((ndp, n)),
        ],
        compiler_params=pltpu.CompilerParams(
            collective_id=0, has_side_effects=True, vmem_limit_bytes=VMEM_LIMIT
        ),
    )(tokens.T, cotangent.T, w_gate, w_up, w_down)
    acts_t, cots, hid_t, dgate, dup = parts
    if kept != share:
        cots = lax.dynamic_slice_in_dim(cots, lax.axis_index("dp") * share, share, 2)
    cots = cots.reshape(count, share)
    dgate, dup = (value.reshape(count, wide) for value in (dgate, dup))
    tile = tile_of(wide)
    strip = pl.BlockSpec((count, tile), lambda j: (0, j))
    tall = pl.BlockSpec((1, share, tile), lambda j: (0, 0, j))
    return pl.pallas_call(
        grads_kernel,
        grid=(wide // tile,),
        in_specs=[
            pl.BlockSpec((share, count), lambda j: (0, 0)),
            pl.BlockSpec((tile, count), lambda j: (j, 0)),
            pl.BlockSpec((count, share), lambda j: (0, 0)),
            strip,
            strip,
        ],
        out_specs=(tall, tall, pl.BlockSpec((1, tile, share), lambda j: (0, j, 0))),
        out_shape=(
            jax.ShapeDtypeStruct((1, share, wide), f32),
            jax.ShapeDtypeStruct((1, share, wide), f32),
            jax.ShapeDtypeStruct((1, wide, share), f32),
        ),
        compiler_params=pltpu.CompilerParams(vmem_limit_bytes=VMEM_LIMIT),
    )(acts_t, hid_t, cots, dgate, dup)


def solution(mesh):
    in_specs = (
        P("dp", "tensor"),
        P("segment", None, "tensor"),
        P("segment", None, "tensor"),
        P("segment", "tensor", None),
        P("dp", "tensor"),
    )
    out_specs = (
        P("segment", "dp", "tensor"),
        P("segment", "dp", "tensor"),
        P("segment", "tensor", "dp"),
    )
    run = functools.partial(local, mesh.shape["tensor"], mesh.shape["dp"])
    return jax.shard_map(run, mesh=mesh, in_specs=in_specs, out_specs=out_specs, check_vma=False)
```
